256 devices in a mesh: ctx: 64 (over z, x, core), grp: 4 (over y).
Axes of the slice: x: 4, y: 4, z: 8, core: 2. Of those that a mesh axis runs over, the one named last changes fastest.
Arguments:
- queries: bfloat16 [131072, 512], P('ctx', 'grp'), may hold values from -100 to 100
- kv_cache: bfloat16 [131072, 256], P(('ctx', 'grp')), may hold values from -6 to 6
- grad_out: bfloat16 [131072, 512], P('ctx', 'grp'), may hold values from -6 to 6
- doc_tiles: int32 [32], replicated, may hold values from 1 to 12, 256 in all
Outputs:
- grad_queries: bfloat16 [131072, 512], P('ctx', 'grp')
- grad_kv: bfloat16 [131072, 256], P(('ctx', 'grp'))
The draws below stay inside these ranges and needn't reach their ends.
All inputs are finite; a program needn't handle non-finite values.
Results may differ from the reference program's by a relative error of at most 0.0059.
Values may be sent and summed in bfloat16 or wider, within the bound.
A program may use at most 64 MiB of HBM per device.

```python
import math
import jax
import jax.numpy as jnp
import numpy as np
from jax import lax

DH = 128
HQ = 4
TILE = 512
MAXT = 12
TOKENS = 131072
NDOCS = 32


def shared_keys(key):
    return jnp.clip(jax.random.normal(key, (TOKENS, DH), jnp.float32), -5.0, 5.0)


def draw_kv_cache(key, part):
    keys = shared_keys(key)
    key = jax.random.fold_in(key, 3)
    values = jnp.clip(jax.random.normal(key, (TOKENS, DH), jnp.float32), -6.0, 6.0)
    return jnp.concatenate([keys, values], axis=1).astype(jnp.bfloat16)


def draw_queries(key, part):
    key = jax.random.fold_in(key, 5)
    queries = jnp.clip(jax.random.normal(key, (TOKENS, HQ * DH), jnp.float32), -6.0, 6.0)
    return queries.astype(jnp.bfloat16)


def steps_of(own_key, dims, shards, smallest, top_value):
    loudness = 1.0
    for axis_at, parts in shards:
        draws = jax.random.uniform(jax.random.fold_in(jax.random.fold_in(own_key, 6), axis_at), (parts,), jnp.float32, smallest / len(shards), top_value / len(shards))
        loudness = loudness * jnp.repeat(jnp.exp(draws), dims[axis_at] // parts).reshape((-1,) + (1,) * (len(dims) - 1 - axis_at))
    return loudness


def length_profile(amount, total, reach, lean):
    portions = [(1 << 20) // math.isqrt(grade ** lean) + 1 for grade in range(2, amount + 1)]
    surplus, counts = total - reach - (amount - 1), [1] * (amount - 1)
    while surplus > 0:
        free = [i for i in range(amount - 1) if counts[i] < reach]
        pool, remaining = sum([portions[i] for i in free]), surplus
        for i in free:
            more = min(reach - counts[i], max(1, remaining * portions[i] // pool), surplus)
            counts[i] = counts[i] + more
            surplus = surplus - more
    return np.array([reach] + counts)


def ragged(stream_key, amount, total, limit, slope):
    if amount == 2:
        one = jax.random.randint(stream_key, (), max(1, total - limit), min(limit, total - 1) + 1)
        return jnp.stack([one, total - one])
    sizes = jnp.asarray(length_profile(amount, total, limit, slope), jnp.int32)
    twos = (amount - 1) // 2
    donor, taker = sizes[1:1 + 2 * twos:2], sizes[2:2 + 2 * twos:2]
    margin = jnp.minimum(donor - 1, limit - taker)
    shifted = jax.random.randint(jax.random.fold_in(stream_key, 1), (twos,), 0, 1 << 20) % (margin + 1)
    sizes = sizes.at[1:1 + 2 * twos:2].set(donor - shifted).at[2:2 + 2 * twos:2].set(taker + shifted)
    return sizes[jax.random.permutation(jax.random.fold_in(stream_key, 2), amount)]


def scatter_about(stream_key, shape, spread, limit, pieces=(), held_as=jnp.bfloat16):
    entries = spread * jax.random.normal(stream_key, shape, jnp.float32)
    if pieces:
        entries = entries * steps_of(stream_key, shape, pieces, -0.22, 0.18)
    return jnp.clip(entries, -limit, limit).astype(held_as)


def setup_inputs(seed: int = 0) -> dict:
    streams_of = jax.random.split(jax.random.key(seed), 5)
    queries = draw_queries(jax.random.fold_in(streams_of[4], 71), 0)
    kv_cache = draw_kv_cache(jax.random.fold_in(streams_of[4], 71), 0)
    grad_out = scatter_about(streams_of[2], (TOKENS, HQ * DH), 1.0, 6.0, ((0, 64), (1, 4)))
    doc_tiles = ragged(streams_of[3], NDOCS, TOKENS // TILE, MAXT, 1).astype(jnp.int32)
    return {"queries": queries, "kv_cache": kv_cache, "grad_out": grad_out, "doc_tiles": doc_tiles}


NEG_FILL = -1e+30

def document_starts(doc_tiles, tile_count):
    doc_ends = jnp.cumsum(doc_tiles).astype(jnp.int32)
    doc_begins = (doc_ends - doc_tiles).astype(jnp.int32)
    tile_ids = jnp.arange(tile_count, dtype=jnp.int32)
    inside = (tile_ids[:, None] >= doc_begins[None, :]) & (tile_ids[:, None] < doc_ends[None, :])
    return lax.optimization_barrier(jnp.sum(jnp.where(inside, doc_begins[None, :], 0), axis=1)).astype(jnp.int32)

def widen(array):
    return array.astype(jnp.float32)

def narrow_keep(array):
    return widen(lax.optimization_barrier(array.astype(jnp.bfloat16)))

def reference(queries, kv_cache, grad_out, doc_tiles):
    tile_count = TOKENS // TILE
    scale = 1.0 / math.sqrt(DH)
    starts = document_starts(doc_tiles, tile_count)
    query_tiles = queries.reshape(tile_count, TILE, HQ, DH)
    grad_tiles = grad_out.reshape(tile_count, TILE, HQ, DH)
    cache_tiles = kv_cache.reshape(tile_count, TILE, 2 * DH)
    row_ids = jnp.arange(TILE, dtype=jnp.int32)
    causal = row_ids[:, None] >= row_ids[None, :]

    def per_tile(grad_cache, inputs):
        q_tile, g_tile, tile_pos = inputs
        first_tile = starts[tile_pos]
        q_wide = widen(q_tile)
        g_wide = widen(g_tile)

        def scores_at(key_pos):
            kv_tile = widen(lax.dynamic_index_in_dim(cache_tiles, key_pos, 0, keepdims=False))
            raw = jnp.einsum('qhd,kd->hqk', q_wide, kv_tile[:, :DH]) * scale
            keep = jnp.logical_or(key_pos != tile_pos, causal)
            return (jnp.where(keep[None], raw, NEG_FILL), kv_tile)

        def first_pass(key_pos, carry):
            row_top, row_total = carry
            scores, _ = scores_at(key_pos)
            new_top = jnp.maximum(row_top, lax.optimization_barrier(jnp.max(scores, axis=2)))
            row_total = row_total * jnp.exp(row_top - new_top) + lax.optimization_barrier(jnp.sum(jnp.exp(scores - new_top[..., None]), axis=2))
            return (new_top, row_total)
        start_carry = (jnp.full((HQ, TILE), NEG_FILL, jnp.float32), jnp.zeros((HQ, TILE), jnp.float32))
        row_top, row_total = lax.fori_loop(first_tile, tile_pos + 1, first_pass, start_carry)
        log_norm = row_top + jnp.log(row_total)

        def second_pass(key_pos, attended):
            scores, kv_tile = scores_at(key_pos)
            probs_low = narrow_keep(jnp.exp(scores - log_norm[..., None]))
            return attended + jnp.einsum('hqk,kd->hqd', probs_low, kv_tile[:, DH:])
        attended = lax.fori_loop(first_tile, tile_pos + 1, second_pass, jnp.zeros((HQ, TILE, DH), jnp.float32))
        delta = jnp.einsum('qhd,hqd->hq', g_wide, attended)

        def third_pass(key_pos, carry):
            grad_q, cache_acc = carry
            scores, kv_tile = scores_at(key_pos)
            probs = jnp.exp(scores - log_norm[..., None])
            probs_low = narrow_keep(probs)
            dprobs = jnp.einsum('qhd,kd->hqk', g_wide, kv_tile[:, DH:])
            dscore = narrow_keep(probs * (dprobs - delta[..., None]))
            grad_q = grad_q + jnp.einsum('hqk,kd->qhd', dscore, kv_tile[:, :DH])
            grad_key = jnp.einsum('hqk,qhd->kd', dscore, q_wide)
            grad_value = jnp.einsum('hqk,qhd->kd', probs_low, g_wide)
            previous = lax.dynamic_index_in_dim(cache_acc, key_pos, 0, keepdims=False)
            updated = previous + jnp.concatenate([grad_key, grad_value], axis=1)
            cache_acc = lax.dynamic_update_index_in_dim(cache_acc, updated, key_pos, 0)
            return (grad_q, cache_acc)
        start_grad = (jnp.zeros((TILE, HQ, DH), jnp.float32), grad_cache)
        grad_q, grad_cache = lax.fori_loop(first_tile, tile_pos + 1, third_pass, start_grad)
        grad_q_low = (grad_q * scale).astype(jnp.bfloat16).reshape(TILE, HQ * DH)
        return (grad_cache, grad_q_low)
    grad_cache = jnp.zeros((tile_count, TILE, 2 * DH), jnp.float32)
    tile_positions = jnp.arange(tile_count, dtype=jnp.int32)
    grad_cache, grad_q_all = lax.scan(per_tile, grad_cache, (query_tiles, grad_tiles, tile_positions))
    grad_queries = grad_q_all.reshape(TOKENS, HQ * DH)
    grad_kv = jnp.concatenate([grad_cache[..., :DH] * scale, grad_cache[..., DH:]], axis=2)
    grad_kv = grad_kv.astype(jnp.bfloat16).reshape(TOKENS, 2 * DH)
    return (grad_queries, grad_kv)
```

```python
import functools
import math

import jax
import jax.numpy as jnp
from jax import lax
from jax.experimental import pallas as pl
from jax.experimental.pallas import tpu as pltpu
from jax.sharding import PartitionSpec as P

DH = 128
TILE = 512
HALF = TILE // 2
LOCAL = 4
WINDOW = 16
SCALE = 1.0 / math.sqrt(DH)
C = SCALE * math.log2(math.e)
LOW = -1e30
f32 = jnp.float32
bf16 = jnp.bfloat16
MESH = pl.DeviceIdType.MESH


def dot(a, b, dims):
    return lax.dot_general(a, b, (dims, ((), ())), preferred_element_type=f32)


NT = ((1,), (1,))
NN = ((1,), (0,))


def document_starts(doc_tiles, tile_count):
    doc_ends = jnp.cumsum(doc_tiles)
    doc_begins = doc_ends - doc_tiles
    tile_ids = jnp.arange(tile_count, dtype=jnp.int32)
    inside = (tile_ids[:, None] >= doc_begins[None, :]) & (tile_ids[:, None] < doc_ends[None, :])
    return jnp.sum(jnp.where(inside, doc_begins[None, :], 0), axis=1)


def kernel(
    ctx_count,
    first_ref, q_ref, g_ref, kv_ref,
    dq_ref, dkv_ref,
    kvw, stage, ddA, ddB, half, full, xin, acc, own, dqt, m_s, l_s, d_s,
    sendG, sendD, sendX, recvA, recvB,
    bsendD, brecvA, brecvB, bsendG, brecvG, bsendX, brecvX,
):
    c = lax.axis_index("ctx")
    y = lax.axis_index("grp")
    k = lax.rem(c, 2)
    other = c + 1 - 2 * k
    yR, yO, yL = (y + 1) % 4, (y + 2) % 4, (y + 3) % 4
    up = lambda n: (c + n) % ctx_count
    down = lambda n: (c + ctx_count - n) % ctx_count

    def remote(src, dst, ssem, rsem, dev):
        return pltpu.make_async_remote_copy(
            src_ref=src, dst_ref=dst, send_sem=ssem, recv_sem=rsem, device_id=dev, device_id_type=MESH
        )

    def landed(ref, sem):
        remote(ref, ref, sem, sem, (other, y)).wait_recv()

    def gone(ref, sem):
        remote(ref, ref, sem, sem, (other, y)).wait_send()

    kvw[12 + y] = kv_ref[...]
    m_s[...] = jnp.full_like(m_s, LOW)
    l_s[...] = jnp.zeros_like(l_s)
    d_s[...] = jnp.zeros_like(d_s)

    barrier = pltpu.get_barrier_semaphore()
    far = (c + ctx_count + 6 * k - 3) % ctx_count
    for dev in ((other, y), (c, yR), (c, yL), (up(2), y), (down(2), y), (far, y)):
        pl.semaphore_signal(barrier, inc=1, device_id=dev, device_id_type=MESH)
    pl.semaphore_wait(barrier, 6)

    def share(group, base):
        src = kvw.at[base + y]
        remote(src, src, sendG.at[group, 0], recvA.at[base + y], (c, yR)).start()
        remote(src, src, sendG.at[group, 1], recvA.at[base + y], (c, yL)).start()

    def relay(group, base):
        landed(kvw.at[base + yL], recvA.at[base + yL])
        top = kvw.at[base + yL, pl.ds(0, HALF)]
        remote(top, top, sendG.at[group, 2], recvA.at[base + yL], (c, yR)).start()
        landed(kvw.at[base + yR], recvA.at[base + yR])
        low = kvw.at[base + yR, pl.ds(HALF, HALF)]
        remote(low, low, sendG.at[group, 3], recvB.at[base + yR], (c, yL)).start()

    def last_in(base):
        landed(kvw.at[base + yO, pl.ds(0, HALF)], recvA.at[base + yO])
        landed(kvw.at[base + yO, pl.ds(HALF, HALF)], recvB.at[base + yO])

    def across(src, dst):
        remote(kvw.at[src], kvw.at[dst], sendD.at[src], recvA.at[dst], (other, y)).start()

    def across_own(u):
        @pl.when(k == 0)
        def _():
            across(12 + u, 8 + u)

    def across_second(u):
        across(4 + u, 8 * k + u)

    share(0, 12)
    mine = kvw.at[12 + y]
    remote(mine, kvw.at[4 + y], sendX.at[0], recvA.at[4 + y], (up(2), y)).start()

    @pl.when(k == 1)
    def _():
        remote(mine, kvw.at[y], sendX.at[1], recvA.at[y], (up(3), y)).start()

    across_own(y)

    causal = lax.broadcasted_iota(jnp.int32, (TILE, TILE), 1) >= lax.broadcasted_iota(
        jnp.int32, (TILE, TILE), 0
    )

    def forward_pair(slot, keys, values, t, diagonal):
        scores = dot(keys, q_ref[t], NT) * C
        if diagonal:
            scores = jnp.where(causal, scores, LOW)
        m = m_s[t]
        valid = first_ref[t] <= slot
        new_m = jnp.where(valid, jnp.maximum(m, jnp.max(scores, axis=0, keepdims=True)), m)
        e = jnp.exp2(scores - jnp.where(valid, new_m, -LOW))
        dp = dot(values, g_ref[t], NT)
        fade = jnp.exp2(m - new_m)
        m_s[t] = new_m
        l_s[t] = l_s[t] * fade + jnp.sum(e, axis=0, keepdims=True)
        d_s[t] = d_s[t] * fade + jnp.sum(e * dp, axis=0, keepdims=True)

    def split(slot):
        tile = kvw[slot]
        return tile[:, :DH], tile[:, DH:]

    def in_order(r):
        return (y + 3 * r - 5 * (r // 2) - 2 * (r // 3) + 4) % 4

    def forward_own(r, carry):
        @pl.when(r == 1)
        def _():
            relay(0, 12)
            across_own(yL)
            across_own(yR)

        @pl.when(r == 2)
        def _():
            landed(kvw.at[4 + y], recvA.at[4 + y])
            share(1, 4)
            across_second(y)

        @pl.when(r == 3)
        def _():
            last_in(12)
            across_own(yO)

            @pl.when(k == 0)
            def _():
                landed(kvw.at[y], recvA.at[y])
                share(2, 0)

        u = in_order(r)
        slot = 12 + u
        forward_pair(slot, *split(slot), u, True)

        def below(t, carry):
            forward_pair(slot, *split(slot), t, False)
            return carry

        return lax.fori_loop(u + 1, LOCAL, below, carry)

    lax.fori_loop(0, 4, forward_own, 0)

    def forward_full(i, carry):
        r = i % 4
        u = in_order(r)
        base = 4 + 4 * ((i // 4 + k) % 2)

        @pl.when(i == 1)
        def _():
            relay(1, 4)
            across_second(yL)
            across_second(yR)

        @pl.when(i == 3)
        def _():
            last_in(4)
            across_second(yO)

        @pl.when(jnp.logical_and(i == 4, k == 0))
        def _():
            relay(2, 0)

        @pl.when(jnp.logical_and(i == 6, k == 0))
        def _():
            last_in(0)

        @pl.when(base == 8)
        def _():
            landed(kvw.at[8 + u], recvA.at[8 + u])

        slot = base + u
        keys, values = split(slot)
        for t in range(LOCAL):
            forward_pair(slot, keys, values, t, False)
        return carry

    lax.fori_loop(0, 8, forward_full, 0)

    def forward_far(r, carry):
        u = in_order(r)

        @pl.when(k == 1)
        def _():
            landed(kvw.at[u], recvA.at[u])

        def above(t, carry):
            forward_pair(u, *split(u), t, False)
            return carry

        return lax.fori_loop(0, u, above, carry)

    lax.fori_loop(0, 4, forward_far, 0)

    for t in range(LOCAL):
        total = l_s[t]
        m_s[t] = m_s[t] + jnp.log2(total)
        d_s[t] = d_s[t] / total
    dqt[...] = jnp.zeros_like(dqt)

    def settle(group, base):
        gone(kvw.at[base + y], sendG.at[group, 0])
        gone(kvw.at[base + y], sendG.at[group, 1])
        gone(kvw.at[base + yL, pl.ds(0, HALF)], sendG.at[group, 2])
        gone(kvw.at[base + yR, pl.ds(HALF, HALF)], sendG.at[group, 3])

    settle(0, 12)
    settle(1, 4)
    gone(mine, sendX.at[0])
    for u in range(4):
        gone(kvw.at[4 + u], sendD.at[4 + u])

    @pl.when(k == 0)
    def _():
        settle(2, 0)
        for u in range(4):
            gone(kvw.at[12 + u], sendD.at[12 + u])

    @pl.when(k == 1)
    def _():
        gone(mine, sendX.at[1])

    def backward_pair(slot, keys, values, keys_t, t, diagonal):
        q, g = q_ref[t], g_ref[t]
        x = dot(keys, q, NT) * C - jnp.where(first_ref[t] <= slot, m_s[t], -LOW)
        if diagonal:
            x = jnp.where(causal, x, LOW)
        p = jnp.exp2(x)
        ds = (p * (dot(values, g, NT) - d_s[t])).astype(bf16)
        dqt[t] += dot(keys_t, ds, NN)
        return dot(ds, q, NN), dot(p.astype(bf16), g, NN)

    def to_y(r):
        return (y + 2 - r + 3 * (r // 2) - 2 * (r // 3) + 4) % 4

    def clear():
        acc[...] = jnp.zeros_like(acc)

    def one_pair(slot, t, diagonal):
        keys, values = split(slot)
        dk, dv = backward_pair(slot, keys, values, keys.astype(f32).T.astype(bf16), t, diagonal)
        acc[:, :DH] += dk
        acc[:, DH:] += dv

    def reduce_step(group, r, u, keep):
        part = stage.at[group, u]

        @pl.when(r == 0)
        def _():
            part[...] = acc[...].astype(bf16)
            remote(
                part.at[pl.ds(0, HALF)], half.at[group, 0],
                bsendG.at[group, 0], brecvG.at[group, 0], (c, yR),
            ).start()
            remote(
                part.at[pl.ds(HALF, HALF)], half.at[group, 1],
                bsendG.at[group, 1], brecvG.at[group, 1], (c, yL),
            ).start()

        @pl.when(r == 1)
        def _():
            landed(half.at[group, 0], brecvG.at[group, 0])
            acc[:HALF] += half[group, 0].astype(f32)
            part[...] = acc[...].astype(bf16)
            remote(part, full.at[group, 0], bsendG.at[group, 2], brecvG.at[group, 2], (c, yR)).start()

        @pl.when(r == 2)
        def _():
            landed(half.at[group, 1], brecvG.at[group, 1])
            acc[HALF:] += half[group, 1].astype(f32)
            part[...] = acc[...].astype(bf16)
            remote(part, full.at[group, 1], bsendG.at[group, 3], brecvG.at[group, 3], (c, yL)).start()

        @pl.when(r == 3)
        def _():
            keep[...] = acc[...]

    def reduced(group, keep):
        landed(full.at[group, 0], brecvG.at[group, 2])
        landed(full.at[group, 1], brecvG.at[group, 3])
        return keep[...] + full[group, 0].astype(f32) + full[group, 1].astype(f32)

    def reduce_gone(group):
        gone(stage.at[group, yO, pl.ds(0, HALF)], bsendG.at[group, 0])
        gone(stage.at[group, yO, pl.ds(HALF, HALF)], bsendG.at[group, 1])
        gone(stage.at[group, yR], bsendG.at[group, 2])
        gone(stage.at[group, yL], bsendG.at[group, 3])

    def backward_far(r, carry):
        u = to_y(r)
        clear()

        def above(t, carry):
            one_pair(u, t, False)
            return carry

        lax.fori_loop(0, u, above, 0)

        @pl.when(k == 0)
        def _():
            reduce_step(2, r, u, own.at[1])

        @pl.when(k == 1)
        def _():
            stage[2, u] = acc[...].astype(bf16)
            remote(stage.at[2, u], ddA.at[u], bsendD.at[0, u], brecvA.at[u], (other, y)).start()

        return carry

    lax.fori_loop(0, 4, backward_far, 0)

    def backward_full(i, carry):
        r = i % 4
        u = to_y(r)
        base = 8 - 4 * (i // 4)
        slot = base + u
        keys, values = split(slot)
        keys_t = keys.T
        dk, dv = backward_pair(slot, keys, values, keys_t, 0, False)
        for t in range(1, LOCAL):
            dk_t, dv_t = backward_pair(slot, keys, values, keys_t, t, False)
            dk += dk_t
            dv += dv_t
        acc[:, :DH] = dk
        acc[:, DH:] = dv

        @pl.when(i < 4)
        def _():
            stage[3, u] = acc[...].astype(bf16)
            remote(stage.at[3, u], ddB.at[u], bsendD.at[1, u], brecvB.at[u], (other, y)).start()

            @pl.when(jnp.logical_and(i == 2, k == 0))
            def _():
                stage[2, y] = reduced(2, own.at[1]).astype(bf16)
                remote(stage.at[2, y], xin.at[1], bsendX.at[1], brecvX.at[1], (down(3), y)).start()

        @pl.when(i >= 4)
        def _():
            @pl.when(k == 0)
            def _():
                landed(ddA.at[u], brecvA.at[u])
                acc[...] += ddA[u].astype(f32)

            @pl.when(k == 1)
            def _():
                landed(ddB.at[u], brecvB.at[u])
                acc[...] += ddB[u].astype(f32)

            reduce_step(1, r, u, own.at[1])

        return carry

    lax.fori_loop(0, 8, backward_full, 0)

    def backward_own(r, carry):
        u = to_y(r)
        slot = 12 + u
        clear()
        one_pair(slot, u, True)

        def below(t, carry):
            one_pair(slot, t, False)
            return carry

        lax.fori_loop(u + 1, LOCAL, below, 0)

        @pl.when(k == 0)
        def _():
            landed(ddB.at[u], brecvB.at[u])
            acc[...] += ddB[u].astype(f32)

        @pl.when(r == 1)
        def _():
            stage[1, y] = reduced(1, own.at[1]).astype(bf16)
            remote(stage.at[1, y], xin.at[0], bsendX.at[0], brecvX.at[0], (down(2), y)).start()

        reduce_step(0, r, u, own.at[0])
        return carry

    lax.fori_loop(0, 4, backward_own, 0)

    for t in range(LOCAL):
        dq_ref[t] = (dqt[t].T * SCALE).astype(bf16)

    landed(xin.at[0], brecvX.at[0])
    own[0] = own[0] + xin[0].astype(f32)

    @pl.when(k == 1)
    def _():
        landed(xin.at[1], brecvX.at[1])
        own[0] = own[0] + xin[1].astype(f32)

    total = reduced(0, own.at[0])
    dkv_ref[:, :DH] = (total[:, :DH] * SCALE).astype(bf16)
    dkv_ref[:, DH:] = total[:, DH:].astype(bf16)

    reduce_gone(0)
    reduce_gone(1)
    gone(stage.at[1, y], bsendX.at[0])
    for u in range(4):
        gone(stage.at[3, u], bsendD.at[1, u])

    @pl.when(k == 0)
    def _():
        reduce_gone(2)
        gone(stage.at[2, y], bsendX.at[1])

    @pl.when(k == 1)
    def _():
        for u in range(4):
            gone(stage.at[2, u], bsendD.at[0, u])


def shards(queries, kv_cache, grad_out, doc_tiles):
    ctx_count = lax.axis_size("ctx")
    c = lax.axis_index("ctx")
    tile_count = ctx_count * LOCAL
    starts = document_starts(doc_tiles, tile_count)
    firsts = lax.dynamic_slice(starts, (c * LOCAL,), (LOCAL,)) - (c * LOCAL - 12)
    firsts = jnp.broadcast_to(firsts[:, None, None], (LOCAL, 1, TILE)).astype(jnp.int32)
    vmem = pl.BlockSpec(memory_space=pltpu.VMEM)
    tile = (TILE, 2 * DH)
    halved = (HALF, 2 * DH)
    row = pltpu.VMEM((LOCAL, 1, TILE), f32)
    dma = pltpu.SemaphoreType.DMA
    dq, dkv = pl.pallas_call(
        functools.partial(kernel, ctx_count),
        out_shape=(
            jax.ShapeDtypeStruct((LOCAL, TILE, DH), bf16),
            jax.ShapeDtypeStruct(tile, bf16),
        ),
        in_specs=[vmem] * 4,
        out_specs=(vmem, vmem),
        scratch_shapes=[
            pltpu.VMEM((WINDOW,) + tile, bf16),
            pltpu.VMEM((4, 4) + tile, bf16),
            pltpu.VMEM((4,) + tile, bf16),
            pltpu.VMEM((4,) + tile, bf16),
            pltpu.VMEM((3, 2) + halved, bf16),
            pltpu.VMEM((3, 2) + tile, bf16),
            pltpu.VMEM((2,) + tile, bf16),
            pltpu.VMEM(tile, f32),
            pltpu.VMEM((2,) + tile, f32),
            pltpu.VMEM((LOCAL, DH, TILE), f32),
            row, row, row,
            dma((3, 4)), dma((WINDOW,)), dma((2,)), dma((WINDOW,)), dma((WINDOW,)),
            dma((2, 4)), dma((4,)), dma((4,)), dma((3, 4)), dma((3, 4)), dma((2,)), dma((2,)),
        ],
        compiler_params=pltpu.CompilerParams(
            collective_id=0, has_side_effects=True, vmem_limit_bytes=56 << 20
        ),
        cost_estimate=pl.CostEstimate(
            flops=48 * 7 * 2 * TILE * TILE * DH,
            bytes_accessed=4 << 20,
            transcendentals=48 * 2 * TILE * TILE,
        ),
        name="attention_backward",
    )(
        firsts,
        queries.reshape(LOCAL, TILE, DH),
        grad_out.reshape(LOCAL, TILE, DH),
        kv_cache,
    )
    return dq.reshape(LOCAL * TILE, DH), dkv


def solution(mesh):
    placed = (P("ctx", "grp"), P(("ctx", "grp"), None), P("ctx", "grp"), P())
    return jax.shard_map(
        shards,
        mesh=mesh,
        in_specs=placed,
        out_specs=(P("ctx", "grp"), P(("ctx", "grp"), None)),
        check_vma=False,
    )
```

```python
import functools
import math

import jax
import jax.numpy as jnp
from jax import lax
from jax.experimental import pallas as pl
from jax.experimental.pallas import tpu as pltpu
from jax.sharding import PartitionSpec as P

DH = 128
TILE = 512
HALF = TILE // 2
LOCAL = 4
WINDOW = 16
SCALE = 1.0 / math.sqrt(DH)
C = SCALE * math.log2(math.e)
LOW = -1e30
f32 = jnp.float32
bf16 = jnp.bfloat16
MESH = pl.DeviceIdType.MESH


def dot(a, b, dims):
    return lax.dot_general(a, b, (dims, ((), ())), preferred_element_type=f32)


NT = ((1,), (1,))
NN = ((1,), (0,))


def kernel(
    ctx_count,
    doc_ref, q_hbm, g_hbm, kv_hbm,
    dq_hbm, dkv_hbm,
    q_ref, g_ref, dq_ref, dkv_ref, local_sem, kvw, stage, ddA, ddB, half, full, xin, acc, own, dqt, m_s, l_s, d_s, first_s,
    e_s, dp_s, top_s, p_all, ds_all,
    sendG, sendD, sendX, recvA, recvB,
    bsendD, brecvA, brecvB, bsendG, brecvG, bsendX, brecvX,
):
    c = lax.axis_index("ctx")
    y = lax.axis_index("grp")
    k = lax.rem(c, 2)
    other = c + 1 - 2 * k
    yR, yO, yL = (y + 1) % 4, (y + 2) % 4, (y + 3) % 4
    up = lambda n: (c + n) % ctx_count
    down = lambda n: (c + ctx_count - n) % ctx_count

    def remote(src, dst, ssem, rsem, dev):
        return pltpu.make_async_remote_copy(
            src_ref=src, dst_ref=dst, send_sem=ssem, recv_sem=rsem, device_id=dev, device_id_type=MESH
        )

    def landed(ref, sem):
        remote(ref, ref, sem, sem, (other, y)).wait_recv()

    def gone(ref, sem):
        remote(ref, ref, sem, sem, (other, y)).wait_send()

    barrier = pltpu.get_barrier_semaphore()
    far = (c + ctx_count + 6 * k - 3) % ctx_count
    for dev in ((other, y), (c, yR), (c, yL), (up(2), y), (down(2), y), (far, y)):
        pl.semaphore_signal(barrier, inc=1, device_id=dev, device_id_type=MESH)

    kv_in = pltpu.make_async_copy(kv_hbm, kvw.at[12 + y], local_sem.at[0])
    q_in = pltpu.make_async_copy(q_hbm, q_ref, local_sem.at[1])
    g_in = pltpu.make_async_copy(g_hbm, g_ref, local_sem.at[2])
    kv_in.start()
    q_in.start()
    g_in.start()

    begin = jnp.int32(0)
    firsts = [jnp.int32(0)] * LOCAL
    for doc in range(doc_ref.shape[0]):
        firsts = [
            jnp.where(begin <= c * LOCAL + t, begin, firsts[t]) for t in range(LOCAL)
        ]
        begin = begin + doc_ref[doc]
    for t in range(LOCAL):
        first_s[t] = jnp.full((1, TILE), firsts[t] - (c * LOCAL - 12), jnp.int32)
    m_s[...] = jnp.full_like(m_s, LOW)
    l_s[...] = jnp.zeros_like(l_s)
    d_s[...] = jnp.zeros_like(d_s)

    kv_in.wait()
    pl.semaphore_wait(barrier, 6)

    def share(group, base):
        src = kvw.at[base + y]
        remote(src, src, sendG.at[group, 0], recvA.at[base + y], (c, yR)).start()
        remote(src, src, sendG.at[group, 1], recvA.at[base + y], (c, yL)).start()

    def relay(group, base):
        landed(kvw.at[base + yL], recvA.at[base + yL])
        top = kvw.at[base + yL, pl.ds(0, HALF)]
        remote(top, top, sendG.at[group, 2], recvA.at[base + yL], (c, yR)).start()
        landed(kvw.at[base + yR], recvA.at[base + yR])
        low = kvw.at[base + yR, pl.ds(HALF, HALF)]
        remote(low, low, sendG.at[group, 3], recvB.at[base + yR], (c, yL)).start()

    def last_in(base):
        landed(kvw.at[base + yO, pl.ds(0, HALF)], recvA.at[base + yO])
        landed(kvw.at[base + yO, pl.ds(HALF, HALF)], recvB.at[base + yO])

    def across(src, dst):
        remote(kvw.at[src], kvw.at[dst], sendD.at[src], recvA.at[dst], (other, y)).start()

    def across_own(u):
        @pl.when(k == 0)
        def _():
            across(12 + u, 8 + u)

    def across_second(u):
        across(4 + u, 8 * k + u)

    share(0, 12)
    mine = kvw.at[12 + y]
    remote(mine, kvw.at[4 + y], sendX.at[0], recvA.at[4 + y], (up(2), y)).start()

    across_own(y)

    causal = lax.broadcasted_iota(jnp.int32, (TILE, TILE), 1) >= lax.broadcasted_iota(
        jnp.int32, (TILE, TILE), 0
    )

    def span(t, end=None):
        return slice(t * TILE, (t + 1 if end is None else end) * TILE)

    def forward_pair(slot, keys, values, t, diagonal, kept):
        scores = dot(keys, q_ref[span(t), :], NT) * C
        if diagonal:
            scores = jnp.where(causal, scores, LOW)
        m = m_s[t]
        valid = first_s[t] <= slot
        new_m = jnp.where(valid, jnp.maximum(m, jnp.max(scores, axis=0, keepdims=True)), m)
        e = jnp.exp2(scores - jnp.where(valid, new_m, -LOW))
        dp = dot(values, g_ref[span(t), :], NT)
        if kept:
            e_s[slot - 4, t] = e.astype(bf16)
            low = dp.astype(bf16)
            dp_s[slot - 4, t] = low
            top_s[slot - 4, t] = new_m
            dp = low.astype(f32)
        fade = jnp.exp2(m - new_m)
        m_s[t] = new_m
        l_s[t] = l_s[t] * fade + jnp.sum(e, axis=0, keepdims=True)
        d_s[t] = d_s[t] * fade + jnp.sum(e * dp, axis=0, keepdims=True)

    def split(slot):
        tile = kvw[slot]
        return tile[:, :DH], tile[:, DH:]

    def in_order(r):
        return (y + 3 * r - 5 * (r // 2) - 2 * (r // 3) + 4) % 4

    def each(u, body):
        for n in range(4):
            pl.when(u == n)(functools.partial(body, n))

    def forward_own(n):
        keys, values = split(12 + n)
        for t in range(n, LOCAL):
            forward_pair(12 + n, keys, values, t, t == n, False)

    def forward_far(n):
        if n:
            keys, values = split(n)
            for t in range(n):
                forward_pair(n, keys, values, t, False, False)

    def forward_step(j, carry):
        is_own = jnp.logical_or(j < 3, j == 5)

        @pl.when(j == 1)
        def _():
            @pl.when(k == 1)
            def _():
                gone(mine, sendX.at[0])
                remote(mine, kvw.at[y], sendX.at[1], recvA.at[y], (up(3), y)).start()

            relay(0, 12)
            across_own(yL)
            across_own(yR)
            landed(kvw.at[4 + y], recvA.at[4 + y])
            share(1, 4)
            across_second(y)

        @pl.when(j == 5)
        def _():
            last_in(12)
            remote(
                kvw.at[12 + yO], kvw.at[4 + yO], sendX.at[2], recvA.at[4 + yO], (up(2), y)
            ).start()
            across_own(yO)

            @pl.when(k == 0)
            def _():
                landed(kvw.at[y], recvA.at[y])
                share(2, 0)

        @pl.when(is_own)
        def _():
            each(in_order(j - 2 * (j // 5)), forward_own)

        @pl.when(jnp.logical_not(is_own))
        def _():
            i = j - 3 - j // 6
            r = i // 2
            u = in_order(r)
            base = 4 + 4 * ((i + k) % 2)

            @pl.when(i == 2)
            def _():
                landed(kvw.at[4 + yL], recvA.at[4 + yL])
                across_second(yL)
                landed(kvw.at[4 + yR], recvA.at[4 + yR])
                across_second(yR)

            @pl.when(i == 6)
            def _():
                landed(kvw.at[4 + yO], recvA.at[4 + yO])
                across_second(yO)

            @pl.when(jnp.logical_and(i == 5, k == 0))
            def _():
                relay(2, 0)

            @pl.when(base == 8)
            def _():
                landed(kvw.at[8 + u], recvA.at[8 + u])

            slot = base + u
            keys, values = split(slot)
            for t in range(LOCAL):
                forward_pair(slot, keys, values, t, False, True)

        return carry

    q_in.wait()
    g_in.wait()
    lax.fori_loop(0, 12, forward_step, 0)

    def forward_last(r, carry):
        u = in_order(r)

        @pl.when(k == 1)
        def _():
            landed(kvw.at[u], recvA.at[u])

        @pl.when(jnp.logical_and(k == 0, r == 3))
        def _():
            last_in(0)

        each(u, forward_far)
        return carry

    lax.fori_loop(0, 4, forward_last, 0)

    for t in range(LOCAL):
        total = l_s[t]
        m_s[t] = m_s[t] + jnp.log2(total)
        d_s[t] = d_s[t] / total
    dqt[...] = jnp.zeros_like(dqt)

    def settle(group, base):
        gone(kvw.at[base + y], sendG.at[group, 0])
        gone(kvw.at[base + y], sendG.at[group, 1])
        gone(kvw.at[base + yL, pl.ds(0, HALF)], sendG.at[group, 2])
        gone(kvw.at[base + yR, pl.ds(HALF, HALF)], sendG.at[group, 3])

    settle(0, 12)
    gone(kvw.at[4 + y], sendG.at[1, 0])
    gone(kvw.at[4 + y], sendG.at[1, 1])
    gone(kvw.at[12 + yO], sendX.at[2])
    for u in range(4):
        gone(kvw.at[4 + u], sendD.at[4 + u])

    @pl.when(k == 0)
    def _():
        settle(2, 0)
        gone(mine, sendX.at[0])
        for u in range(4):
            gone(kvw.at[12 + u], sendD.at[12 + u])

    @pl.when(k == 1)
    def _():
        gone(mine, sendX.at[1])

    def kept_pair(slot, t):
        p = e_s[slot - 4, t].astype(f32) * jnp.exp2(top_s[slot - 4, t] - m_s[t])
        ds_all[:, span(t)] = (p * (dp_s[slot - 4, t].astype(f32) - d_s[t])).astype(bf16)
        p_all[:, span(t)] = p.astype(bf16)

    def fresh_pair(slot, keys, values, t, diagonal):
        x = dot(keys, q_ref[span(t), :], NT) * C - jnp.where(first_s[t] <= slot, m_s[t], -LOW)
        if diagonal:
            x = jnp.where(causal, x, LOW)
        p = jnp.exp2(x)
        dp = dot(values, g_ref[span(t), :], NT)
        ds_all[:, span(t)] = (p * (dp - d_s[t])).astype(bf16)
        p_all[:, span(t)] = p.astype(bf16)

    def products(keys_t, begin, end):
        rows = span(begin, end)
        acc[:, :DH] = dot(ds_all[:, rows], q_ref[rows, :], NN)
        acc[:, DH:] = dot(p_all[:, rows], g_ref[rows, :], NN)
        dqt[:, rows] += dot(keys_t, ds_all[:, rows], NN)

    def turned(keys):
        return keys.astype(f32).T.astype(bf16)

    def backward_kept(slot):
        keys_t = turned(kvw[slot][:, :DH])
        for t in range(LOCAL):
            kept_pair(slot, t)
        products(keys_t, 0, LOCAL)

    def backward_far(n):
        if n == 0:
            acc[...] = jnp.zeros_like(acc)
        else:
            keys, values = split(n)
            for t in range(n):
                fresh_pair(n, keys, values, t, False)
            products(turned(keys), 0, n)

    def backward_own(n):
        keys, values = split(12 + n)
        for t in range(n, LOCAL):
            fresh_pair(12 + n, keys, values, t, t == n)
        products(turned(keys), n, LOCAL)

    def to_y(r):
        return (y + 2 - r + 3 * (r // 2) - 2 * (r // 3) + 4) % 4

    def send_halves(group):
        part = stage.at[group, yO]
        remote(
            part.at[pl.ds(0, HALF)], half.at[group, 0],
            bsendG.at[group, 0], brecvG.at[group, 0], (c, yR),
        ).start()
        remote(
            part.at[pl.ds(HALF, HALF)], half.at[group, 1],
            bsendG.at[group, 1], brecvG.at[group, 1], (c, yL),
        ).start()

    def send_right(group):
        part = stage.at[group, yR]
        remote(part, full.at[group, 0], bsendG.at[group, 2], brecvG.at[group, 2], (c, yR)).start()

    def send_left(group):
        part = stage.at[group, yL]
        remote(part, full.at[group, 1], bsendG.at[group, 3], brecvG.at[group, 3], (c, yL)).start()

    def reduce_step(group, r, keep):
        @pl.when(r == 0)
        def _():
            stage[group, yO] = acc[...].astype(bf16)
            send_halves(group)

        @pl.when(r == 1)
        def _():
            landed(half.at[group, 0], brecvG.at[group, 0])
            acc[:HALF] += half[group, 0].astype(f32)
            stage[group, yR] = acc[...].astype(bf16)
            send_right(group)

        @pl.when(r == 2)
        def _():
            landed(half.at[group, 1], brecvG.at[group, 1])
            acc[HALF:] += half[group, 1].astype(f32)
            stage[group, yL] = acc[...].astype(bf16)
            send_left(group)

        @pl.when(r == 3)
        def _():
            keep[...] = acc[...]

    def second_step(r):
        @pl.when(r == 0)
        def _():
            stage[1, yO] = acc[...].astype(bf16)
            remote(stage.at[1, yO], xin.at[2], bsendX.at[2], brecvX.at[2], (down(2), y)).start()

        @pl.when(r == 1)
        def _():
            stage[1, yR] = acc[...].astype(bf16)
            send_right(1)

        @pl.when(r == 2)
        def _():
            stage[1, yL] = acc[...].astype(bf16)
            send_left(1)

        @pl.when(r == 3)
        def _():
            own[1] = acc[...]

    def reduced(group, keep):
        landed(full.at[group, 0], brecvG.at[group, 2])
        landed(full.at[group, 1], brecvG.at[group, 3])
        return keep[...] + full[group, 0].astype(f32) + full[group, 1].astype(f32)

    def reduce_gone(group):
        if group == 1:
            gone(stage.at[1, yO], bsendX.at[2])
        else:
            gone(stage.at[group, yO, pl.ds(0, HALF)], bsendG.at[group, 0])
            gone(stage.at[group, yO, pl.ds(HALF, HALF)], bsendG.at[group, 1])
        gone(stage.at[group, yR], bsendG.at[group, 2])
        gone(stage.at[group, yL], bsendG.at[group, 3])

    def backward_first(r, carry):
        u = to_y(r)
        each(u, backward_far)

        @pl.when(jnp.logical_and(k == 0, r < 3))
        def _():
            stage[2, u] = acc[...].astype(bf16)

            @pl.when(r == 0)
            def _():
                send_halves(2)

        @pl.when(jnp.logical_and(k == 0, r == 3))
        def _():
            own[1] = acc[...]

        @pl.when(k == 1)
        def _():
            stage[2, u] = acc[...].astype(bf16)
            remote(stage.at[2, u], ddA.at[u], bsendD.at[0, u], brecvA.at[u], (other, y)).start()

        return carry

    lax.fori_loop(0, 4, backward_first, 0)

    def early(r):
        u = to_y(r)
        backward_kept(8 + u)
        stage[3, u] = acc[...].astype(bf16)
        remote(stage.at[3, u], ddB.at[u], bsendD.at[1, u], brecvB.at[u], (other, y)).start()

        @pl.when(jnp.logical_and(r == 0, k == 0))
        def _():
            landed(half.at[2, 0], brecvG.at[2, 0])
            stage[2, yR, :HALF] += half[2, 0]
            send_right(2)
            landed(half.at[2, 1], brecvG.at[2, 1])
            stage[2, yL, HALF:] += half[2, 1]
            send_left(2)

        @pl.when(jnp.logical_and(r == 2, k == 0))
        def _():
            stage[2, y] = reduced(2, own.at[1]).astype(bf16)
            remote(stage.at[2, y], xin.at[1], bsendX.at[1], brecvX.at[1], (down(3), y)).start()

        backward_kept(4 + u)

        @pl.when(k == 0)
        def _():
            landed(ddA.at[u], brecvA.at[u])
            acc[...] += ddA[u].astype(f32)

        @pl.when(k == 1)
        def _():
            landed(ddB.at[u], brecvB.at[u])
            acc[...] += ddB[u].astype(f32)

        second_step(r)

    def late(r):
        u = to_y(r)
        each(u, backward_own)

        @pl.when(k == 0)
        def _():
            landed(ddB.at[u], brecvB.at[u])
            acc[...] += ddB[u].astype(f32)

        @pl.when(r == 0)
        def _():
            landed(xin.at[2], brecvX.at[2])
            acc[...] += xin[2].astype(f32)

        reduce_step(0, r, own.at[0])

        @pl.when(r == 1)
        def _():
            stage[1, y] = reduced(1, own.at[1]).astype(bf16)
            remote(stage.at[1, y], xin.at[0], bsendX.at[0], brecvX.at[0], (down(2), y)).start()

    def backward_step(r, carry):
        pl.when(r < 4)(functools.partial(early, r))
        pl.when(r >= 2)(functools.partial(late, r - 2))
        return carry

    lax.fori_loop(0, 6, backward_step, 0)

    for t in range(LOCAL):
        dq_ref[span(t), :] = (dqt[:, span(t)].T * SCALE).astype(bf16)
    dq_out = pltpu.make_async_copy(dq_ref, dq_hbm, local_sem.at[1])
    dq_out.start()

    landed(xin.at[0], brecvX.at[0])
    own[0] = own[0] + xin[0].astype(f32)

    @pl.when(k == 1)
    def _():
        landed(xin.at[1], brecvX.at[1])
        own[0] = own[0] + xin[1].astype(f32)

    total = reduced(0, own.at[0])
    dkv_ref[:, :DH] = (total[:, :DH] * SCALE).astype(bf16)
    dkv_ref[:, DH:] = total[:, DH:].astype(bf16)
    dkv_out = pltpu.make_async_copy(dkv_ref, dkv_hbm, local_sem.at[0])
    dkv_out.start()

    reduce_gone(0)
    reduce_gone(1)
    gone(stage.at[1, y], bsendX.at[0])
    for u in range(4):
        gone(stage.at[3, u], bsendD.at[1, u])

    @pl.when(k == 0)
    def _():
        reduce_gone(2)
        gone(stage.at[2, y], bsendX.at[1])

    @pl.when(k == 1)
    def _():
        for u in range(4):
            gone(stage.at[2, u], bsendD.at[0, u])
    dq_out.wait()
    dkv_out.wait()


def hand_over(dq_in, dkv_in, dq_out, dkv_out, dq_mid, dkv_mid, sem):
    legs = []
    for source, middle, target, parts in ((dq_in, dq_mid, dq_out, 4), (dkv_in, dkv_mid, dkv_out, 2)):
        rows = source.shape[0] // parts
        for n in range(parts):
            block = pl.ds(n * rows, rows)
            number = len(legs)
            legs.append((
                pltpu.make_async_copy(source.at[block], middle.at[block], sem.at[0, number]),
                pltpu.make_async_copy(middle.at[block], target.at[block], sem.at[1, number]),
            ))
    for fetch, _ in legs:
        fetch.start()
    for fetch, put in legs:
        fetch.wait()
        put.start()
    for _, put in legs:
        put.wait()


def shards(queries, kv_cache, grad_out, doc_tiles):
    ctx_count = lax.axis_size("ctx")
    anywhere = pl.BlockSpec(memory_space=pl.ANY)
    rows = pltpu.VMEM((LOCAL * TILE, DH), bf16)
    tile = (TILE, 2 * DH)
    halved = (HALF, 2 * DH)
    row = pltpu.VMEM((LOCAL, 1, TILE), f32)
    dma = pltpu.SemaphoreType.DMA
    dq, dkv = pl.pallas_call(
        functools.partial(kernel, ctx_count),
        out_shape=(
            jax.ShapeDtypeStruct((LOCAL * TILE, DH), bf16),
            jax.ShapeDtypeStruct(tile, bf16),
        ),
        in_specs=[pl.BlockSpec(memory_space=pltpu.SMEM)] + [anywhere] * 3,
        out_specs=(anywhere, anywhere),
        scratch_shapes=[
            rows, rows, rows,
            pltpu.VMEM(tile, bf16),
            pltpu.SemaphoreType.DMA((3,)),
            pltpu.VMEM((WINDOW,) + tile, bf16),
            pltpu.VMEM((4, 4) + tile, bf16),
            pltpu.VMEM((4,) + tile, bf16),
            pltpu.VMEM((4,) + tile, bf16),
            pltpu.VMEM((3, 2) + halved, bf16),
            pltpu.VMEM((3, 2) + tile, bf16),
            pltpu.VMEM((3,) + tile, bf16),
            pltpu.VMEM(tile, f32),
            pltpu.VMEM((2,) + tile, f32),
            pltpu.VMEM((DH, LOCAL * TILE), f32),
            row, row, row,
            pltpu.VMEM((LOCAL, 1, TILE), jnp.int32),
            pltpu.VMEM((8, LOCAL, TILE, TILE), bf16),
            pltpu.VMEM((8, LOCAL, TILE, TILE), bf16),
            pltpu.VMEM((8, LOCAL, 1, TILE), f32),
            pltpu.VMEM((TILE, LOCAL * TILE), bf16),
            pltpu.VMEM((TILE, LOCAL * TILE), bf16),
            dma((3, 4)), dma((WINDOW,)), dma((3,)), dma((WINDOW,)), dma((WINDOW,)),
            dma((2, 4)), dma((4,)), dma((4,)), dma((3, 4)), dma((3, 4)), dma((3,)), dma((3,)),
        ],
        compiler_params=pltpu.CompilerParams(
            collective_id=0, has_side_effects=True, vmem_limit_bytes=60 << 20
        ),
        cost_estimate=pl.CostEstimate(
            flops=48 * 7 * 2 * TILE * TILE * DH,
            bytes_accessed=4 << 20,
            transcendentals=48 * 2 * TILE * TILE,
        ),
        name="attention_backward",
    )(
        doc_tiles, queries, grad_out, kv_cache,
    )
    return pl.pallas_call(
        hand_over,
        out_shape=(
            jax.ShapeDtypeStruct(dq.shape, bf16),
            jax.ShapeDtypeStruct(dkv.shape, bf16),
        ),
        in_specs=[anywhere] * 2,
        out_specs=(anywhere, anywhere),
        scratch_shapes=[rows, pltpu.VMEM(tile, bf16), dma((2, 6))],
        name="hand_over",
    )(dq, dkv)


def solution(mesh):
    placed = (P("ctx", "grp"), P(("ctx", "grp"), None), P("ctx", "grp"), P())
    return jax.shard_map(
        shards,
        mesh=mesh,
        in_specs=placed,
        out_specs=(P("ctx", "grp"), P(("ctx", "grp"), None)),
        check_vma=False,
    )
```
